128 devices in a mesh: rep: 4 (over z), con: 32 (over y, x, core).
Axes of the slice: x: 4, y: 4, z: 4, core: 2. Of those that a mesh axis runs over, the one named last changes fastest.
Arguments:
- amplitudes: bfloat16 [4, 8, 100, 16000], P(None, None, None, ('rep', 'con')), may hold values from -8 to 8
- block_table: int32 [4, 8], replicated, may hold values 0 or 1
- intermediate: bfloat16 [4, 16000, 16000], P(None, 'rep', 'con'), may hold values from -0.046875 to 0.046875
- slab_energy: float32 [8], replicated, may hold values from -1 to -0.3
- slab_irrep: int32 [8], replicated, may hold values from 0 to 7
- occ_energy: float32 [8, 20], replicated, may hold values from -1 to -0.3
- virt_energy: float32 [8, 100], replicated, may hold values from 0.1 to 1.5
Outputs:
- update: bfloat16 [4, 8, 100, 16000], P(None, 'rep', None, 'con')
The draws below stay inside these ranges and needn't reach their ends.
All inputs are finite; a program needn't handle non-finite values.
Results may differ from the reference program's by a relative error of at most 0.001.
Values may be sent and summed in bfloat16 or wider, within the bound.
No kernel may reach another device: no remote copies, remote signals or barrier semaphores. Data moves between devices by JAX's collectives and lax.ppermute only.
A program may use at most 192 MiB of HBM per device.

```python
import jax
import jax.numpy as jnp

IRREPS = 8
OCC_IRR = 20
VIRT_IRR = 100
BLOCKS = 4
SLAB = 8
PAIRS = 16000


def set_ends(drawn, own_key, least, largest):
    place = [jax.random.randint(jax.random.fold_in(own_key, axis), (), 0, length) for axis, length in enumerate(drawn.shape)]
    main_axis = drawn.shape.index(max(drawn.shape))
    next_to = place[:main_axis] + [(place[main_axis] + 1) % drawn.shape[main_axis]] + place[main_axis + 1:]
    return drawn.at[tuple(place)].set(least).at[tuple(next_to)].set(largest)


def level_of(rng, extent, shards, least, top_value):
    def one(position, blocks):
        steps = jax.random.uniform(jax.random.fold_in(jax.random.fold_in(rng, 6), position), (blocks,), jnp.float32, least / len(shards), top_value / len(shards))
        return jnp.repeat(jnp.exp(steps), extent[position] // blocks).reshape((-1,) + (1,) * (len(extent) - position - 1))

    level = one(*shards[0])
    for cut in shards[1:]:
        level = level * one(*cut)
    return level


def scatter_about(key, extent, spread, most, pieces=(), kind=jnp.bfloat16):
    entries = jax.random.normal(key, extent, jnp.float32) * spread
    if len(pieces) > 0:
        entries = level_of(key, extent, pieces, -0.22, 0.18) * entries
    return jnp.clip(entries, min=-most, max=most).astype(kind)


def setup_inputs(seed: int = 0) -> dict:
    streams_of = jax.random.split(jax.random.key(seed), 8)
    return {
        "amplitudes": scatter_about(streams_of[0], (BLOCKS, SLAB, VIRT_IRR, PAIRS), 2.0, 8.0, ((3, 128),)),
        "block_table": set_ends((jax.random.randint(streams_of[1], (BLOCKS, IRREPS), 0, 4) < 3).astype(jnp.int32), jax.random.fold_in(streams_of[1], 1), 0, 1),
        "intermediate": scatter_about(streams_of[2], (BLOCKS, PAIRS, PAIRS), PAIRS ** -0.5, 0.046875, ((1, 4), (2, 32))),
        "slab_energy": jnp.clip(jax.random.uniform(streams_of[3], (SLAB,), jnp.float32, -1.0, -0.3), -1.0, -0.3),
        "slab_irrep": set_ends(jax.random.randint(streams_of[4], (SLAB,), 0, IRREPS), jax.random.fold_in(streams_of[4], 1), 0, IRREPS - 1).astype(jnp.int32),
        "occ_energy": jnp.clip(jax.random.uniform(streams_of[5], (IRREPS, OCC_IRR), jnp.float32, -1.0, -0.3), -1.0, -0.3),
        "virt_energy": jnp.clip(jax.random.uniform(streams_of[6], (IRREPS, VIRT_IRR), jnp.float32, 0.1, 1.5), 0.1, 1.5),
    }


def reference(amplitudes, block_table, intermediate, slab_energy, slab_irrep, occ_energy, virt_energy):
    columns = jnp.arange(PAIRS, dtype=jnp.int32)
    col_irrep = columns // (OCC_IRR * VIRT_IRR)
    keep = block_table[:, col_irrep].astype(jnp.bfloat16)
    masked = amplitudes * keep[:, None, None, :]
    cycle_list = []
    for block in range(BLOCKS):
        flat = masked[block].reshape(SLAB * VIRT_IRR, PAIRS)
        cycle_list.append(jnp.dot(flat, intermediate[block], preferred_element_type=jnp.float32).reshape(SLAB, VIRT_IRR, PAIRS))
    cycle = jnp.stack(cycle_list, 0)
    block_ids = jnp.arange(BLOCKS, dtype=jnp.int32)
    a_irrep = jnp.bitwise_xor(slab_irrep[None, :], block_ids[:, None])
    energy_a = virt_energy[a_irrep]
    pair_index = columns // VIRT_IRR
    virt_index = columns % VIRT_IRR
    pair_irrep = pair_index // OCC_IRR
    energy_j = occ_energy.reshape(-1)[pair_index]
    b_irrep = jnp.bitwise_xor(pair_irrep[None, :], block_ids[:, None])
    energy_b = virt_energy[b_irrep, virt_index[None, :]]
    denominator = slab_energy[None, :, None, None] + energy_j[None, None, None, :] - energy_a[:, :, :, None] - energy_b[:, None, None, :]
    return (cycle / denominator).astype(jnp.bfloat16)
```

```python
import functools

import jax
import jax.numpy as jnp
from jax import lax
from jax.experimental import pallas as pl
from jax.experimental.pallas import tpu as pltpu
from jax.sharding import PartitionSpec as P

SIDE = 4
SHARD = 128
COLS = 512
OFFSETS = (0, -1, 1, 2)
PARTS = (((0, 200),), ((0, 104), (104, 200)))
STEPS = 64.0
LEAST = 2.0**-125
TOP = 32766.0
PARAMS = pltpu.CompilerParams(vmem_limit_bytes=24 * 1024 * 1024)


def ring_pairs(stage, hop):
    pairs = []
    for y in range(SIDE):
        for x in range(SIDE):
            for core in range(2):
                if (core + stage) % 2 == 0:
                    to_x, to_y = (x + hop) % SIDE, y
                else:
                    to_x, to_y = x, (y + hop) % SIDE
                pairs.append(((y * SIDE + x) * 2 + core, (to_y * SIDE + to_x) * 2 + core))
    return pairs


def ring(value, stage, hop):
    return lax.ppermute(value, "con", ring_pairs(stage, hop))


def swap_cores(value):
    return lax.ppermute(value, "con", [(i, i ^ 1) for i in range(2 * SIDE * SIDE)])


def to_replica(value, hop):
    return lax.ppermute(value, "rep", [(i, (i + hop) % SIDE) for i in range(SIDE)])


def code_rows(acc, table, own, codes):
    _, _, rows, cols = acc.shape
    lane = lax.broadcasted_iota(jnp.int32, (rows, cols), 1)
    for side in range(2):
        own[side] = acc[side, table[17]]
        for hop, code in enumerate(codes):
            value = acc[side, table[18 + hop]]
            most = jnp.maximum(jnp.max(jnp.abs(value), axis=1, keepdims=True), LEAST)
            level = jnp.ceil(jnp.log2(most) * STEPS)
            scaled = value * jnp.exp2(level * (-1.0 / STEPS)) * TOP
            code[side] = jnp.where(lane == cols - 1, level, jnp.round(scaled)).astype(jnp.int32).astype(jnp.int16)


def product_kernel(
    h, chip_cols, table, t0, t1, t2, t3, w_own, w_other, own, code1, code2, code3, t_buf, w_buf, acc, t_sem, w_sem
):
    _, reps, rows, cols = acc.shape
    depth, width = w_own.shape[1:]
    chips = t_buf.shape[0]
    block = table[16] * 2 + h
    edges = [-(-chip_cols * SIDE * g // 16) * 16 for g in range(SIDE)] + [depth]
    w_copies = []
    for g in range(SIDE):
        span = pl.ds(edges[g], edges[g + 1] - edges[g])
        for side, w in enumerate((w_own, w_other)):
            w_copies.append(pltpu.make_async_copy(w.at[block, span], w_buf.at[side, span], w_sem.at[g, side]))
    for copy in w_copies[:2]:
        copy.start()
    for j, t_ref in enumerate((t0, t1, t2, t3)):
        for i in range(SIDE):
            chip = table[j * SIDE + i]
            pltpu.make_async_copy(t_ref.at[i], t_buf.at[chip], t_sem.at[chip]).start()
    for copy in w_copies[2:]:
        copy.start()
    tail = w_buf.shape[1] - depth
    for side in range(2):
        w_buf[side, depth:, :] = jnp.zeros((tail, width), w_buf.dtype)
    for g in range(SIDE):
        group = range(g * SIDE, (g + 1) * SIDE)
        for copy in w_copies[2 * g : 2 * g + 2]:
            copy.wait()
        for chip in group:
            pltpu.make_async_copy(t0.at[0], t_buf.at[chip], t_sem.at[chip]).wait()
        left = jnp.concatenate([t_buf[chip] for chip in group], axis=1)
        for side in range(2):
            windows = [w_buf[side, chip * chip_cols : chip * chip_cols + 2 * SHARD, :] for chip in group]
            part = jnp.dot(left, jnp.concatenate(windows, axis=0), preferred_element_type=jnp.float32)
            part = part.reshape(reps, rows, width)
            if g == 0:
                acc[side, :, :, width:] = jnp.zeros((reps, rows, cols - width), jnp.float32)
                acc[side, :, :, :width] = part
            else:
                acc[side, :, :, :width] += part
    code_rows(acc, table, own, (code1, code2, code3))


def multiply(table, h, chip_cols, t_parts, w_own, w_other):
    count, rows4, lanes = t_parts[0].shape
    rows = rows4 // SIDE
    depth, width = w_own.shape[1:]
    chips = SIDE * count
    code_shape = (2, rows, COLS)
    whole = pl.BlockSpec(memory_space=pl.ANY)
    return pl.pallas_call(
        functools.partial(product_kernel, h, chip_cols),
        grid_spec=pltpu.PrefetchScalarGridSpec(
            num_scalar_prefetch=1,
            grid=(1,),
            in_specs=[whole] * 6,
            out_specs=[pl.BlockSpec(code_shape, lambda k, tab: (0, 0, 0))] * 4,
            scratch_shapes=[
                pltpu.VMEM((chips, rows4, lanes), jnp.bfloat16),
                pltpu.VMEM((2, depth + 16, width), jnp.bfloat16),
                pltpu.VMEM((2, SIDE, rows, COLS), jnp.float32),
                pltpu.SemaphoreType.DMA((chips,)),
                pltpu.SemaphoreType.DMA((SIDE, 2)),
            ],
        ),
        out_shape=[jax.ShapeDtypeStruct(code_shape, jnp.float32)] + [jax.ShapeDtypeStruct(code_shape, jnp.int16)] * 3,
        compiler_params=PARAMS,
        cost_estimate=pl.CostEstimate(
            flops=2 * rows4 * depth * 2 * width, bytes_accessed=2 * depth * width * 2 * 3, transcendentals=0
        ),
    )(table, *t_parts, w_own, w_other)


def finish_kernel(own, code1, code2, code3, rows_e, cols_e, out_own, out_other):
    cols = own.shape[2]
    for side, out in enumerate((out_own, out_other)):
        total = own[side]
        for code in (code1, code2, code3):
            whole = code[side].astype(jnp.int32).astype(jnp.float32)
            level = whole[:, cols - 1 :]
            total = total + whole * (jnp.exp2(level * (1.0 / STEPS)) * (1.0 / TOP))
        denominator = rows_e[:, 0:1] + cols_e[side, 0:1, :] - rows_e[:, 1:2] - cols_e[side, 1:2, :]
        out[...] = (total / denominator).astype(jnp.bfloat16)[:, : out.shape[1]]


def finish(own, codes, rows_e, cols_e, width):
    rows = own.shape[1]
    return pl.pallas_call(
        finish_kernel,
        out_shape=[jax.ShapeDtypeStruct((rows, width), jnp.bfloat16)] * 2,
        compiler_params=PARAMS,
        cost_estimate=pl.CostEstimate(flops=10 * own.size, bytes_accessed=2_000_000, transcendentals=0),
    )(own, *codes, rows_e, cols_e)


def row_energies(my_h, slab_energy, slab_irrep, virt_energy):
    irreps = virt_energy.shape[0]
    here = slab_energy.shape[0] // SIDE
    start = lax.axis_index("rep") * here
    energy_i = lax.dynamic_slice_in_dim(slab_energy, start, here)
    labels = lax.dynamic_slice_in_dim(slab_irrep, start, here)
    a_irrep = jnp.bitwise_xor(labels[None, :], my_h[:, None])
    hits = a_irrep[:, :, None] == jnp.arange(irreps, dtype=jnp.int32)
    energy_a = jnp.sum(jnp.where(hits[..., None], virt_energy[None, None], 0.0), axis=2)
    energy_i = jnp.broadcast_to(energy_i[None, :, None], energy_a.shape)
    return jnp.stack([energy_i, energy_a], axis=3).reshape(my_h.shape[0], -1, 2)


def col_energies(my_h, con, width, occ_energy, virt_energy):
    irreps, occ_width = occ_energy.shape
    virt_width = virt_energy.shape[1]
    columns = con * width + jnp.arange(COLS, dtype=jnp.int32)
    pair_index = columns // virt_width
    virt_index = columns % virt_width
    pair_irrep = pair_index // occ_width
    hits_j = pair_index[:, None] == jnp.arange(irreps * occ_width, dtype=jnp.int32)
    energy_j = jnp.sum(jnp.where(hits_j, occ_energy.reshape(-1), 0.0), axis=1)
    b_index = jnp.bitwise_xor(pair_irrep[None, :], my_h[:, None]) * virt_width + virt_index[None, :]
    hits_b = b_index[..., None] == jnp.arange(irreps * virt_width, dtype=jnp.int32)
    energy_b = jnp.sum(jnp.where(hits_b, virt_energy.reshape(-1), 0.0), axis=2)
    inside = jnp.arange(COLS) < width
    energy_j = jnp.broadcast_to(jnp.where(inside, energy_j, -1.0)[None], energy_b.shape)
    return jnp.stack([energy_j, energy_b], axis=1)


def shards(amplitudes, block_table, intermediate, slab_energy, slab_irrep, occ_energy, virt_energy):
    blocks, slab, virt, shard = amplitudes.shape
    width = intermediate.shape[2]
    rows = slab * virt
    per_rep = rows // SIDE
    mine = blocks // 2
    rep, con = lax.axis_index("rep"), lax.axis_index("con")
    core, chip = con % 2, con // 2
    y, x = chip // SIDE, chip % SIDE
    pair_width = occ_energy.shape[1] * virt_energy.shape[1]

    group = (rep * 2 * SIDE * SIDE + con) * shard // pair_width
    keep = lax.dynamic_index_in_dim(block_table, group, axis=1, keepdims=False).astype(jnp.bfloat16)
    masked = amplitudes * keep[:, None, None, None]
    masked = masked.reshape(blocks, rows, shard)
    kept = lax.dynamic_slice_in_dim(masked, core * mine, mine)
    given = lax.dynamic_slice_in_dim(masked, (1 - core) * mine, mine)
    got = swap_cores(given)
    t = jnp.where(core == 0, jnp.concatenate([kept, got], axis=2), jnp.concatenate([got, kept], axis=2))
    t = jnp.pad(t, ((0, 0), (0, 0), (0, 2 * SHARD - 2 * shard)))
    w_other = swap_cores(intermediate)

    near = (jnp.array(OFFSETS, jnp.int32)[None, :], jnp.array(OFFSETS, jnp.int32)[:, None])
    x_chip = jnp.where(core == 0, near[0], near[1])
    y_chip = jnp.where(core == 0, near[1], near[0])
    chips = jnp.mod(y + y_chip, SIDE) * SIDE + jnp.mod(x + x_chip, SIDE)
    table = jnp.concatenate(
        [chips.reshape(-1), core[None], jnp.mod(rep + jnp.arange(SIDE, dtype=jnp.int32), SIDE)]
    ).astype(jnp.int32)

    my_h = core * mine + jnp.arange(mine, dtype=jnp.int32)
    rows_e = row_energies(my_h, slab_energy, slab_irrep, virt_energy)
    cols_e = jnp.stack(
        [col_energies(my_h, c, width, occ_energy, virt_energy) for c in (con, jnp.bitwise_xor(con, 1))], axis=1
    )

    kept, got = [], []
    for h in range(mine):
        before, after = ring(t[h], 0, 1), ring(t[h], 0, -1)
        hop = 1 if h == 0 else -1
        far = ring(before if h == 0 else after, 0, hop)
        row = jnp.stack([t[h], before, after, far]).reshape(SIDE, SIDE, per_rep, 2 * SHARD)
        for first, last in PARTS[h]:
            here = row[:, :, first:last].reshape(SIDE, -1, 2 * SHARD)
            row_before, row_after = ring(here, 1, 1), ring(here, 1, -1)
            row_far = ring(row_before if h == 0 else row_after, 1, hop)
            t_parts = (here, row_before, row_after, row_far)
            own, *codes = multiply(table, h, 2 * shard, t_parts, intermediate, w_other)
            codes = [to_replica(code, hops + 1) for hops, code in enumerate(codes)]
            out_own, out_other = finish(own, codes, rows_e[h, first:last], cols_e[h], width)
            kept.append(out_own)
            got.append(swap_cores(out_other))

    kept, got = jnp.concatenate(kept), jnp.concatenate(got)
    out = jnp.where(core == 0, jnp.concatenate([kept, got]), jnp.concatenate([got, kept]))
    return out.reshape(blocks, slab // SIDE, virt, width)


def solution(mesh):
    placed = (P(None, None, None, ("rep", "con")), P(), P(None, "rep", "con"), P(), P(), P(), P())
    return jax.shard_map(
        shards, mesh=mesh, in_specs=placed, out_specs=P(None, "rep", None, "con"), check_vma=False
    )
```

```python
import functools

import jax
import jax.numpy as jnp
from jax import lax
from jax.experimental import pallas as pl
from jax.experimental.pallas import tpu as pltpu
from jax.sharding import PartitionSpec as P

SIDE = 4
SHARD = 128
COLS = 512
OFFSETS = (0, -1, 1, 2)
CHUNKS = ((0, 0, 112), (1, 0, 112), (0, 112, 200), (1, 112, 200))
TIES = {
    "all1": ("own0",),
    "all2": ("own1",),
    "all3": ("own2",),
    "code33": ("code11",),
    "end0": ("own3",),
    "end1": ("own3",),
    "end2": ("own3",),
    "far2": ("own0",),
    "far3": ("code10", "own1"),
    "minus2": ("minus0", "plus0"),
    "minus3": ("minus1", "plus1"),
    "plus2": ("minus0", "plus0"),
    "plus3": ("minus1", "plus1"),
}
STEPS = 64.0
LEAST = 2.0**-125
TOP = 32766.0
PARAMS = pltpu.CompilerParams(vmem_limit_bytes=40 * 1024 * 1024)


def ring_pairs(stage, hop):
    pairs = []
    for y in range(SIDE):
        for x in range(SIDE):
            for core in range(2):
                if (core + stage) % 2 == 0:
                    to_x, to_y = (x + hop) % SIDE, y
                else:
                    to_x, to_y = x, (y + hop) % SIDE
                pairs.append(((y * SIDE + x) * 2 + core, (to_y * SIDE + to_x) * 2 + core))
    return pairs


def ring(value, stage, hop):
    return lax.ppermute(value, "con", ring_pairs(stage, hop))


def swap_cores(value):
    return lax.ppermute(value, "con", [(i, i ^ 1) for i in range(2 * SIDE * SIDE)])


def to_replica(value, hop):
    return lax.ppermute(value, "rep", [(i, (i + hop) % SIDE) for i in range(SIDE)])


def after(value, *others):
    return lax.optimization_barrier((value, *others))[0]


def code_rows(acc, table, own, codes):
    _, _, rows, cols = acc.shape
    lane = lax.broadcasted_iota(jnp.int32, (rows, cols), 1)
    for side in range(2):
        own[side] = acc[side, table[17]]
        for hop, code in enumerate(codes):
            value = acc[side, table[18 + hop]]
            most = jnp.maximum(jnp.max(jnp.abs(value), axis=1, keepdims=True), LEAST)
            level = jnp.ceil(jnp.log2(most) * STEPS)
            scaled = value * jnp.exp2(level * (-1.0 / STEPS)) * TOP
            code[side] = jnp.where(lane == cols - 1, level, jnp.round(scaled)).astype(jnp.int32).astype(jnp.int16)


def product_kernel(
    h, chip_cols, table, t0, t1, t2, t3, w_own, w_other, own, code1, code2, code3, t_buf, w_buf, acc, t_sem, w_sem
):
    _, reps, rows, cols = acc.shape
    depth, width = w_own.shape[1:]
    block = table[16] * 2 + h
    groups = [(0, 2), (2, 4), (4, 8), (8, 12), (12, 16)]
    over = 2 * SHARD - chip_cols
    edges = [0] + [-(-(chip_cols * low + over) // 16) * 16 for low, _ in groups[1:]] + [depth]
    t_refs = (t0, t1, t2, t3)
    w_copies = []
    for g, (low, high) in enumerate(groups):
        for chip in range(low, high):
            place = table[21 + chip]
            j, i = place // SIDE, place % SIDE
            for arrival, t_ref in enumerate(t_refs):

                @pl.when(j == arrival)
                def _():
                    pltpu.make_async_copy(t_ref.at[i], t_buf.at[chip], t_sem.at[chip]).start()

        span = pl.ds(edges[g], edges[g + 1] - edges[g])
        for side, w in enumerate((w_own, w_other)):
            copy = pltpu.make_async_copy(w.at[block, span], w_buf.at[side, span], w_sem.at[g, side])
            copy.start()
            w_copies.append(copy)
    tail = w_buf.shape[1] - depth
    for side in range(2):
        w_buf[side, depth:, :] = jnp.zeros((tail, width), w_buf.dtype)
    for g, (low, high) in enumerate(groups):
        group = range(low, high)
        for copy in w_copies[2 * g : 2 * g + 2]:
            copy.wait()
        for chip in group:
            pltpu.make_async_copy(t0.at[0], t_buf.at[chip], t_sem.at[chip]).wait()
        left = jnp.concatenate([t_buf[chip] for chip in group], axis=1)
        for side in range(2):
            windows = [w_buf[side, chip * chip_cols : chip * chip_cols + 2 * SHARD, :] for chip in group]
            part = jnp.dot(left, jnp.concatenate(windows, axis=0), preferred_element_type=jnp.float32)
            part = part.reshape(reps, rows, width)
            if g == 0:
                acc[side, :, :, width:] = jnp.zeros((reps, rows, cols - width), jnp.float32)
                acc[side, :, :, :width] = part
            else:
                acc[side, :, :, :width] += part
    code_rows(acc, table, own, (code1, code2, code3))


def multiply(table, h, chip_cols, t_parts, w_own, w_other):
    count, rows4, lanes = t_parts[0].shape
    rows = rows4 // SIDE
    depth, width = w_own.shape[1:]
    chips = SIDE * count
    code_shape = (2, rows, COLS)
    whole = pl.BlockSpec(memory_space=pl.ANY)
    return pl.pallas_call(
        functools.partial(product_kernel, h, chip_cols),
        grid_spec=pltpu.PrefetchScalarGridSpec(
            num_scalar_prefetch=1,
            grid=(1,),
            in_specs=[whole] * 6,
            out_specs=[pl.BlockSpec(code_shape, lambda k, tab: (0, 0, 0))] * 4,
            scratch_shapes=[
                pltpu.VMEM((chips, rows4, lanes), jnp.bfloat16),
                pltpu.VMEM((2, depth + 16, width), jnp.bfloat16),
                pltpu.VMEM((2, SIDE, rows, COLS), jnp.float32),
                pltpu.SemaphoreType.DMA((chips,)),
                pltpu.SemaphoreType.DMA((5, 2)),
            ],
        ),
        out_shape=[jax.ShapeDtypeStruct(code_shape, jnp.float32)] + [jax.ShapeDtypeStruct(code_shape, jnp.int16)] * 3,
        compiler_params=PARAMS,
        cost_estimate=pl.CostEstimate(
            flops=2 * rows4 * depth * 2 * width, bytes_accessed=2 * depth * width * 2 * 3, transcendentals=0
        ),
    )(table, *t_parts, w_own, w_other)


def finish_kernel(own, code1, code2, code3, rows_e, cols_e, out_own, out_other):
    cols = own.shape[2]
    for side, out in enumerate((out_own, out_other)):
        total = own[side]
        for code in (code1, code2, code3):
            whole = code[side].astype(jnp.int32).astype(jnp.float32)
            level = whole[:, cols - 1 :]
            total = total + whole * (jnp.exp2(level * (1.0 / STEPS)) * (1.0 / TOP))
        denominator = rows_e[:, 0:1] + cols_e[side, 0:1, :] - rows_e[:, 1:2] - cols_e[side, 1:2, :]
        out[...] = (total / denominator).astype(jnp.bfloat16)[:, : out.shape[1]]


def finish(own, codes, rows_e, cols_e, width):
    rows = own.shape[1]
    return pl.pallas_call(
        finish_kernel,
        out_shape=[jax.ShapeDtypeStruct((rows, width), jnp.bfloat16)] * 2,
        compiler_params=PARAMS,
        cost_estimate=pl.CostEstimate(flops=10 * own.size, bytes_accessed=2_000_000, transcendentals=0),
    )(own, *codes, rows_e, cols_e)


def row_energies(my_h, slab_energy, slab_irrep, virt_energy):
    irreps = virt_energy.shape[0]
    here = slab_energy.shape[0] // SIDE
    start = lax.axis_index("rep") * here
    energy_i = lax.dynamic_slice_in_dim(slab_energy, start, here)
    labels = lax.dynamic_slice_in_dim(slab_irrep, start, here)
    a_irrep = jnp.bitwise_xor(labels[None, :], my_h[:, None])
    hits = a_irrep[:, :, None] == jnp.arange(irreps, dtype=jnp.int32)
    energy_a = jnp.sum(jnp.where(hits[..., None], virt_energy[None, None], 0.0), axis=2)
    energy_i = jnp.broadcast_to(energy_i[None, :, None], energy_a.shape)
    return jnp.stack([energy_i, energy_a], axis=3).reshape(my_h.shape[0], -1, 2)


def col_energies(my_h, con, width, occ_energy, virt_energy):
    irreps, occ_width = occ_energy.shape
    virt_width = virt_energy.shape[1]
    columns = con * width + jnp.arange(COLS, dtype=jnp.int32)
    pair_index = columns // virt_width
    virt_index = columns % virt_width
    pair_irrep = pair_index // occ_width
    hits_j = pair_index[:, None] == jnp.arange(irreps * occ_width, dtype=jnp.int32)
    energy_j = jnp.sum(jnp.where(hits_j, occ_energy.reshape(-1), 0.0), axis=1)
    b_index = jnp.bitwise_xor(pair_irrep[None, :], my_h[:, None]) * virt_width + virt_index[None, :]
    hits_b = b_index[..., None] == jnp.arange(irreps * virt_width, dtype=jnp.int32)
    energy_b = jnp.sum(jnp.where(hits_b, virt_energy.reshape(-1), 0.0), axis=2)
    inside = jnp.arange(COLS) < width
    energy_j = jnp.broadcast_to(jnp.where(inside, energy_j, -1.0)[None], energy_b.shape)
    return jnp.stack([energy_j, energy_b], axis=1)


def place_of(core, y, x):
    chip = jnp.arange(SIDE * SIDE, dtype=jnp.int32)
    hop_y, hop_x = jnp.mod(chip // SIDE - y, SIDE), jnp.mod(chip % SIDE - x, SIDE)

    def slot(hop):
        return jnp.where(hop == 0, 0, jnp.where(hop == 1, 2, jnp.where(hop == 2, 3, 1)))

    first, second = jnp.where(core == 0, hop_x, hop_y), jnp.where(core == 0, hop_y, hop_x)
    return slot(second) * SIDE + slot(first)


def shards(amplitudes, block_table, intermediate, slab_energy, slab_irrep, occ_energy, virt_energy):
    blocks, slab, virt, shard = amplitudes.shape
    width = intermediate.shape[2]
    rows = slab * virt
    per_rep = rows // SIDE
    mine = blocks // 2
    rep, con = lax.axis_index("rep"), lax.axis_index("con")
    core, chip = con % 2, con // 2
    y, x = chip // SIDE, chip % SIDE
    pair_width = occ_energy.shape[1] * virt_energy.shape[1]

    group = (rep * 2 * SIDE * SIDE + con) * shard // pair_width
    keep = lax.dynamic_index_in_dim(block_table, group, axis=1, keepdims=False).astype(jnp.bfloat16)
    masked = amplitudes * keep[:, None, None, None]
    masked = masked.reshape(blocks, rows, shard)
    kept = lax.dynamic_slice_in_dim(masked, core * mine, mine)
    given = lax.dynamic_slice_in_dim(masked, (1 - core) * mine, mine)
    got = swap_cores(given)
    intermediate = after(intermediate, got)
    t = jnp.where(core == 0, jnp.concatenate([kept, got], axis=2), jnp.concatenate([got, kept], axis=2))
    t = jnp.pad(t, ((0, 0), (0, 0), (0, 2 * SHARD - 2 * shard)))
    near = (jnp.array(OFFSETS, jnp.int32)[None, :], jnp.array(OFFSETS, jnp.int32)[:, None])
    x_chip = jnp.where(core == 0, near[0], near[1])
    y_chip = jnp.where(core == 0, near[1], near[0])
    chips = jnp.mod(y + y_chip, SIDE) * SIDE + jnp.mod(x + x_chip, SIDE)
    table = jnp.concatenate(
        [chips.reshape(-1), core[None], jnp.mod(rep + jnp.arange(SIDE, dtype=jnp.int32), SIDE), place_of(core, y, x)]
    ).astype(jnp.int32)

    my_h = core * mine + jnp.arange(mine, dtype=jnp.int32)
    rows_e = row_energies(my_h, slab_energy, slab_irrep, virt_energy)
    cols_e = jnp.stack(
        [col_energies(my_h, c, width, occ_energy, virt_energy) for c in (con, jnp.bitwise_xor(con, 1))], axis=1
    )

    table = after(table, rows_e, cols_e)
    known = {}

    def tied(name, value):
        return after(value, *[node(other) for other in TIES[name]]) if name in TIES else value

    def node(name):
        if name not in known:
            known[name] = build(name)
        return known[name]

    def build(name):
        kind, k = name[:-1], int(name[-1])
        if kind == "w":
            return swap_cores(tied(name, intermediate))
        if kind == "t":
            return t[k]
        if kind == "both":
            return ring(tied(name, t), 0, 1 if k == 0 else -1)
        if kind == "side":
            return ring(tied(name, node(f"both{k}")[k]), 0, 1 if k == 0 else -1)
        if kind == "row":
            row = jnp.stack([t[k], node("both0")[k], node("both1")[k], node(f"side{k}")])
            return row.reshape(SIDE, SIDE, per_rep, 2 * SHARD)
        h, first, last = CHUNKS[k]
        if kind == "here":
            return node(f"row{h}")[:, :, first:last].reshape(SIDE, -1, 2 * SHARD)
        if kind == "plus":
            return ring(tied(name, node(f"here{k}")), 1, 1)
        if kind == "minus":
            return ring(tied(name, node(f"here{k}")), 1, -1)
        if kind == "far":
            return ring(tied(name, node(f"plus{k}" if h == 0 else f"minus{k}")), 1, 1 if h == 0 else -1)
        if kind == "all":
            parts = [node(f"{part}{k}") for part in ("here", "plus", "minus", "far")]
            return multiply(tied(name, table), h, 2 * shard, parts, intermediate, node("w0"))
        if kind == "own":
            return node(f"all{k}")[0]
        if kind[:-1] == "code":
            hop = int(kind[-1])
            return to_replica(tied(name, node(f"all{k}")[hop]), hop)
        codes = [node(f"code{hop}{k}") for hop in (1, 2, 3)]
        return finish(tied(name, node(f"own{k}")), codes, rows_e[h, first:last], cols_e[h], width)

    done = {}
    for k, (h, first, last) in enumerate(CHUNKS):
        out_own, out_other = node(f"end{k}")
        done[h, first] = out_own, swap_cores(out_other)
    kept, got = [done[key][0] for key in sorted(done)], [done[key][1] for key in sorted(done)]
    kept, got = jnp.concatenate(kept), jnp.concatenate(got)
    out = jnp.where(core == 0, jnp.concatenate([kept, got]), jnp.concatenate([got, kept]))
    return out.reshape(blocks, slab // SIDE, virt, width)


def solution(mesh):
    placed = (P(None, None, None, ("rep", "con")), P(), P(None, "rep", "con"), P(), P(), P(), P())
    return jax.shard_map(
        shards, mesh=mesh, in_specs=placed, out_specs=P(None, "rep", None, "con"), check_vma=False
    )
```

```python
import functools

import jax
import jax.numpy as jnp
from jax import lax
from jax.experimental import pallas as pl
from jax.experimental.pallas import tpu as pltpu
from jax.sharding import PartitionSpec as P

SIDE = 4
SHARD = 128
COLS = 512
OFFSETS = (0, -1, 1, 2)
CHUNKS = ((0, 0, 112), (1, 0, 112), (0, 112, 200), (1, 112, 200))
TIES = {
    "all1": ("own0",),
    "all2": ("own1",),
    "all3": ("own2",),
    "code33": ("code11",),
    "end0": ("own3",),
    "end1": ("own3",),
    "end2": ("own3",),
    "far2": ("own0",),
    "far3": ("code10", "own1"),
    "minus2": ("minus0", "plus0"),
    "minus3": ("minus1", "plus1"),
    "plus2": ("minus0", "plus0"),
    "plus3": ("minus1", "plus1"),
}
STEPS = 64.0
LEAST = 2.0**-125
TOP = 32766.0
PARAMS = pltpu.CompilerParams(vmem_limit_bytes=40 * 1024 * 1024)


def ring_pairs(stage, hop):
    pairs = []
    for y in range(SIDE):
        for x in range(SIDE):
            for core in range(2):
                if (core + stage) % 2 == 0:
                    to_x, to_y = (x + hop) % SIDE, y
                else:
                    to_x, to_y = x, (y + hop) % SIDE
                pairs.append(((y * SIDE + x) * 2 + core, (to_y * SIDE + to_x) * 2 + core))
    return pairs


def ring(value, stage, hop):
    return lax.ppermute(value, "con", ring_pairs(stage, hop))


def swap_cores(value):
    return lax.ppermute(value, "con", [(i, i ^ 1) for i in range(2 * SIDE * SIDE)])


def to_replica(value, hop):
    return lax.ppermute(value, "rep", [(i, (i + hop) % SIDE) for i in range(SIDE)])


def after(value, *others):
    return lax.optimization_barrier((value, *others))[0]


def code_rows(acc, table, own, codes):
    _, _, rows, cols = acc.shape
    lane = lax.broadcasted_iota(jnp.int32, (rows, cols), 1)
    for side in range(2):
        own[side] = acc[side, table[17]]
        for hop, code in enumerate(codes):
            value = acc[side, table[18 + hop]]
            most = jnp.maximum(jnp.max(jnp.abs(value), axis=1, keepdims=True), LEAST)
            level = jnp.ceil(jnp.log2(most) * STEPS)
            scaled = value * jnp.exp2(level * (-1.0 / STEPS)) * TOP
            code[side] = jnp.where(lane == cols - 1, level, jnp.round(scaled)).astype(jnp.int32).astype(jnp.int16)


def product_kernel(
    h, chip_cols, table, t0, t1, t2, t3, w_own, w_other, own, code1, code2, code3, t_buf, w_buf, acc, t_sem, w_sem
):
    _, reps, rows, cols = acc.shape
    depth, width = w_own.shape[1:]
    chips = t_buf.shape[0]
    block = table[16] * 2 + h
    over = 2 * SHARD - chip_cols
    edges = [0] + [-(-(chip_cols * SIDE * g + over) // 16) * 16 for g in range(1, SIDE)] + [depth]
    w_copies = []
    for g in range(SIDE):
        span = pl.ds(edges[g], edges[g + 1] - edges[g])
        for side, w in enumerate((w_own, w_other)):
            w_copies.append(pltpu.make_async_copy(w.at[block, span], w_buf.at[side, span], w_sem.at[g, side]))
    for copy in w_copies[:2]:
        copy.start()
    for j, t_ref in enumerate((t0, t1, t2, t3)):
        for i in range(SIDE):
            chip = table[j * SIDE + i]
            pltpu.make_async_copy(t_ref.at[i], t_buf.at[chip], t_sem.at[chip]).start()
    for copy in w_copies[2:]:
        copy.start()
    tail = w_buf.shape[1] - depth
    for side in range(2):
        w_buf[side, depth:, :] = jnp.zeros((tail, width), w_buf.dtype)
    for g in range(SIDE):
        group = range(g * SIDE, (g + 1) * SIDE)
        for copy in w_copies[2 * g : 2 * g + 2]:
            copy.wait()
        for chip in group:
            pltpu.make_async_copy(t0.at[0], t_buf.at[chip], t_sem.at[chip]).wait()
        left = jnp.concatenate([t_buf[chip] for chip in group], axis=1)
        for side in range(2):
            windows = [w_buf[side, chip * chip_cols : chip * chip_cols + 2 * SHARD, :] for chip in group]
            part = jnp.dot(left, jnp.concatenate(windows, axis=0), preferred_element_type=jnp.float32)
            part = part.reshape(reps, rows, width)
            if g == 0:
                acc[side, :, :, width:] = jnp.zeros((reps, rows, cols - width), jnp.float32)
                acc[side, :, :, :width] = part
            else:
                acc[side, :, :, :width] += part
    code_rows(acc, table, own, (code1, code2, code3))


def multiply(table, h, chip_cols, t_parts, w_own, w_other):
    count, rows4, lanes = t_parts[0].shape
    rows = rows4 // SIDE
    depth, width = w_own.shape[1:]
    chips = SIDE * count
    code_shape = (2, rows, COLS)
    whole = pl.BlockSpec(memory_space=pl.ANY)
    return pl.pallas_call(
        functools.partial(product_kernel, h, chip_cols),
        grid_spec=pltpu.PrefetchScalarGridSpec(
            num_scalar_prefetch=1,
            grid=(1,),
            in_specs=[whole] * 6,
            out_specs=[pl.BlockSpec(code_shape, lambda k, tab: (0, 0, 0))] * 4,
            scratch_shapes=[
                pltpu.VMEM((chips, rows4, lanes), jnp.bfloat16),
                pltpu.VMEM((2, depth + 16, width), jnp.bfloat16),
                pltpu.VMEM((2, SIDE, rows, COLS), jnp.float32),
                pltpu.SemaphoreType.DMA((chips,)),
                pltpu.SemaphoreType.DMA((SIDE, 2)),
            ],
        ),
        out_shape=[jax.ShapeDtypeStruct(code_shape, jnp.float32)] + [jax.ShapeDtypeStruct(code_shape, jnp.int16)] * 3,
        compiler_params=PARAMS,
        cost_estimate=pl.CostEstimate(
            flops=2 * rows4 * depth * 2 * width, bytes_accessed=2 * depth * width * 2 * 3, transcendentals=0
        ),
    )(table, *t_parts, w_own, w_other)


def finish_kernel(own, code1, code2, code3, rows_e, cols_e, out_own, out_other):
    cols = own.shape[2]
    for side, out in enumerate((out_own, out_other)):
        total = own[side]
        for code in (code1, code2, code3):
            whole = code[side].astype(jnp.int32).astype(jnp.float32)
            level = whole[:, cols - 1 :]
            total = total + whole * (jnp.exp2(level * (1.0 / STEPS)) * (1.0 / TOP))
        denominator = rows_e[:, 0:1] + cols_e[side, 0:1, :] - rows_e[:, 1:2] - cols_e[side, 1:2, :]
        out[...] = (total / denominator).astype(jnp.bfloat16)[:, : out.shape[1]]


def finish(own, codes, rows_e, cols_e, width):
    rows = own.shape[1]
    return pl.pallas_call(
        finish_kernel,
        out_shape=[jax.ShapeDtypeStruct((rows, width), jnp.bfloat16)] * 2,
        compiler_params=PARAMS,
        cost_estimate=pl.CostEstimate(flops=10 * own.size, bytes_accessed=2_000_000, transcendentals=0),
    )(own, *codes, rows_e, cols_e)


def row_energies(my_h, slab_energy, slab_irrep, virt_energy):
    irreps = virt_energy.shape[0]
    here = slab_energy.shape[0] // SIDE
    start = lax.axis_index("rep") * here
    energy_i = lax.dynamic_slice_in_dim(slab_energy, start, here)
    labels = lax.dynamic_slice_in_dim(slab_irrep, start, here)
    a_irrep = jnp.bitwise_xor(labels[None, :], my_h[:, None])
    hits = a_irrep[:, :, None] == jnp.arange(irreps, dtype=jnp.int32)
    energy_a = jnp.sum(jnp.where(hits[..., None], virt_energy[None, None], 0.0), axis=2)
    energy_i = jnp.broadcast_to(energy_i[None, :, None], energy_a.shape)
    return jnp.stack([energy_i, energy_a], axis=3).reshape(my_h.shape[0], -1, 2)


def col_energies(my_h, con, width, occ_energy, virt_energy):
    irreps, occ_width = occ_energy.shape
    virt_width = virt_energy.shape[1]
    columns = con * width + jnp.arange(COLS, dtype=jnp.int32)
    pair_index = columns // virt_width
    virt_index = columns % virt_width
    pair_irrep = pair_index // occ_width
    hits_j = pair_index[:, None] == jnp.arange(irreps * occ_width, dtype=jnp.int32)
    energy_j = jnp.sum(jnp.where(hits_j, occ_energy.reshape(-1), 0.0), axis=1)
    b_index = jnp.bitwise_xor(pair_irrep[None, :], my_h[:, None]) * virt_width + virt_index[None, :]
    hits_b = b_index[..., None] == jnp.arange(irreps * virt_width, dtype=jnp.int32)
    energy_b = jnp.sum(jnp.where(hits_b, virt_energy.reshape(-1), 0.0), axis=2)
    inside = jnp.arange(COLS) < width
    energy_j = jnp.broadcast_to(jnp.where(inside, energy_j, -1.0)[None], energy_b.shape)
    return jnp.stack([energy_j, energy_b], axis=1)


def shards(amplitudes, block_table, intermediate, slab_energy, slab_irrep, occ_energy, virt_energy):
    blocks, slab, virt, shard = amplitudes.shape
    width = intermediate.shape[2]
    rows = slab * virt
    per_rep = rows // SIDE
    mine = blocks // 2
    rep, con = lax.axis_index("rep"), lax.axis_index("con")
    core, chip = con % 2, con // 2
    y, x = chip // SIDE, chip % SIDE
    pair_width = occ_energy.shape[1] * virt_energy.shape[1]

    group = (rep * 2 * SIDE * SIDE + con) * shard // pair_width
    keep = lax.dynamic_index_in_dim(block_table, group, axis=1, keepdims=False).astype(jnp.bfloat16)
    masked = amplitudes * keep[:, None, None, None]
    masked = masked.reshape(blocks, rows, shard)
    kept = lax.dynamic_slice_in_dim(masked, core * mine, mine)
    given = lax.dynamic_slice_in_dim(masked, (1 - core) * mine, mine)
    got = swap_cores(given)
    intermediate = after(intermediate, got)
    t = jnp.where(core == 0, jnp.concatenate([kept, got], axis=2), jnp.concatenate([got, kept], axis=2))
    t = jnp.pad(t, ((0, 0), (0, 0), (0, 2 * SHARD - 2 * shard)))
    near = (jnp.array(OFFSETS, jnp.int32)[None, :], jnp.array(OFFSETS, jnp.int32)[:, None])
    x_chip = jnp.where(core == 0, near[0], near[1])
    y_chip = jnp.where(core == 0, near[1], near[0])
    chips = jnp.mod(y + y_chip, SIDE) * SIDE + jnp.mod(x + x_chip, SIDE)
    table = jnp.concatenate(
        [chips.reshape(-1), core[None], jnp.mod(rep + jnp.arange(SIDE, dtype=jnp.int32), SIDE)]
    ).astype(jnp.int32)

    my_h = core * mine + jnp.arange(mine, dtype=jnp.int32)
    rows_e = row_energies(my_h, slab_energy, slab_irrep, virt_energy)
    cols_e = jnp.stack(
        [col_energies(my_h, c, width, occ_energy, virt_energy) for c in (con, jnp.bitwise_xor(con, 1))], axis=1
    )

    table = after(table, rows_e, cols_e)
    known = {}

    def tied(name, value):
        return after(value, *[node(other) for other in TIES[name]]) if name in TIES else value

    def node(name):
        if name not in known:
            known[name] = build(name)
        return known[name]

    def build(name):
        kind, k = name[:-1], int(name[-1])
        if kind == "w":
            return swap_cores(tied(name, intermediate))
        if kind == "t":
            return t[k]
        if kind == "both":
            return ring(tied(name, t), 0, 1 if k == 0 else -1)
        if kind == "side":
            return ring(tied(name, node(f"both{k}")[k]), 0, 1 if k == 0 else -1)
        if kind == "row":
            row = jnp.stack([t[k], node("both0")[k], node("both1")[k], node(f"side{k}")])
            return row.reshape(SIDE, SIDE, per_rep, 2 * SHARD)
        h, first, last = CHUNKS[k]
        if kind == "here":
            return node(f"row{h}")[:, :, first:last].reshape(SIDE, -1, 2 * SHARD)
        if kind == "plus":
            return ring(tied(name, node(f"here{k}")), 1, 1)
        if kind == "minus":
            return ring(tied(name, node(f"here{k}")), 1, -1)
        if kind == "far":
            return ring(tied(name, node(f"plus{k}" if h == 0 else f"minus{k}")), 1, 1 if h == 0 else -1)
        if kind == "all":
            parts = [node(f"{part}{k}") for part in ("here", "plus", "minus", "far")]
            return multiply(tied(name, table), h, 2 * shard, parts, intermediate, node("w0"))
        if kind == "own":
            return node(f"all{k}")[0]
        if kind[:-1] == "code":
            hop = int(kind[-1])
            return to_replica(tied(name, node(f"all{k}")[hop]), hop)
        codes = [node(f"code{hop}{k}") for hop in (1, 2, 3)]
        return finish(tied(name, node(f"own{k}")), codes, rows_e[h, first:last], cols_e[h], width)

    done = {}
    for k, (h, first, last) in enumerate(CHUNKS):
        out_own, out_other = node(f"end{k}")
        done[h, first] = out_own, swap_cores(out_other)
    kept, got = [done[key][0] for key in sorted(done)], [done[key][1] for key in sorted(done)]
    kept, got = jnp.concatenate(kept), jnp.concatenate(got)
    out = jnp.where(core == 0, jnp.concatenate([kept, got]), jnp.concatenate([got, kept]))
    return out.reshape(blocks, slab // SIDE, virt, width)


def solution(mesh):
    placed = (P(None, None, None, ("rep", "con")), P(), P(None, "rep", "con"), P(), P(), P(), P())
    return jax.shard_map(
        shards, mesh=mesh, in_specs=placed, out_specs=P(None, "rep", None, "con"), check_vma=False
    )
```

```python
import functools

import jax
import jax.numpy as jnp
from jax import lax
from jax.experimental import pallas as pl
from jax.experimental.pallas import tpu as pltpu
from jax.sharding import PartitionSpec as P

SIDE = 4
SHARD = 128
COLS = 512
OFFSETS = (0, -1, 1, 2)
CHUNKS = ((0, 0, 112), (1, 0, 112), (0, 112, 200), (1, 112, 200))
TIES = {
    "all1": ("own0",),
    "all2": ("own1",),
    "all3": ("own2",),
    "code33": ("code11",),
    "end0": ("own3",),
    "end1": ("own3",),
    "end2": ("own3",),
    "far2": ("own0",),
    "far3": ("code10", "own1"),
    "minus2": ("minus0", "plus0"),
    "minus3": ("minus1", "plus1"),
    "plus2": ("minus0", "plus0"),
    "plus3": ("minus1", "plus1"),
}
STEPS = 64.0
LEAST = 2.0**-125
TOP = 32766.0
PARAMS = pltpu.CompilerParams(vmem_limit_bytes=40 * 1024 * 1024)


def ring_pairs(stage, hop):
    pairs = []
    for y in range(SIDE):
        for x in range(SIDE):
            for core in range(2):
                if (core + stage) % 2 == 0:
                    to_x, to_y = (x + hop) % SIDE, y
                else:
                    to_x, to_y = x, (y + hop) % SIDE
                pairs.append(((y * SIDE + x) * 2 + core, (to_y * SIDE + to_x) * 2 + core))
    return pairs


def ring(value, stage, hop):
    return lax.ppermute(value, "con", ring_pairs(stage, hop))


def swap_cores(value):
    return lax.ppermute(value, "con", [(i, i ^ 1) for i in range(2 * SIDE * SIDE)])


def to_replica(value, hop):
    return lax.ppermute(value, "rep", [(i, (i + hop) % SIDE) for i in range(SIDE)])


def after(value, *others):
    return lax.optimization_barrier((value, *others))[0]


def code_rows(acc, table, own, codes):
    _, _, rows, cols = acc.shape
    lane = lax.broadcasted_iota(jnp.int32, (rows, cols), 1)
    for side in range(2):
        own[side] = acc[side, table[17]]
        for hop, code in enumerate(codes):
            value = acc[side, table[18 + hop]]
            most = jnp.maximum(jnp.max(jnp.abs(value), axis=1, keepdims=True), LEAST)
            level = jnp.ceil(jnp.log2(most) * STEPS)
            scaled = value * jnp.exp2(level * (-1.0 / STEPS)) * TOP
            code[side] = jnp.where(lane == cols - 1, level, jnp.round(scaled)).astype(jnp.int32).astype(jnp.int16)


def product_kernel(
    h, chip_cols, table, t0, t1, t2, t3, w_own, w_other, own, code1, code2, code3, t_buf, w_buf, acc, t_sem, w_sem
):
    _, reps, rows, cols = acc.shape
    depth, width = w_own.shape[1:]
    chips = t_buf.shape[0]
    block = table[16] * 2 + h
    over = 2 * SHARD - chip_cols
    groups = ((0, 2), (2, 4), (4, 8), (8, 12), (12, 16))
    edges = [0] + [-(-(chip_cols * low + over) // 16) * 16 for low, _ in groups[1:]] + [depth]
    w_copies = []
    for g in range(len(groups)):
        span = pl.ds(edges[g], edges[g + 1] - edges[g])
        for side, w in enumerate((w_own, w_other)):
            w_copies.append(pltpu.make_async_copy(w.at[block, span], w_buf.at[side, span], w_sem.at[g, side]))
    for copy in w_copies[:2]:
        copy.start()
    for j, t_ref in enumerate((t0, t1, t2, t3)):
        for i in range(SIDE):
            chip = table[j * SIDE + i]
            pltpu.make_async_copy(t_ref.at[i], t_buf.at[chip], t_sem.at[chip]).start()
    for copy in w_copies[2:]:
        copy.start()
    tail = w_buf.shape[1] - depth
    for side in range(2):
        w_buf[side, depth:, :] = jnp.zeros((tail, width), w_buf.dtype)
    for g, (low, high) in enumerate(groups):
        group = range(low, high)
        for copy in w_copies[2 * g : 2 * g + 2]:
            copy.wait()
        for chip in group:
            pltpu.make_async_copy(t0.at[0], t_buf.at[chip], t_sem.at[chip]).wait()
        left = jnp.concatenate([t_buf[chip] for chip in group], axis=1)
        for side in range(2):
            windows = [w_buf[side, chip * chip_cols : chip * chip_cols + 2 * SHARD, :] for chip in group]
            part = jnp.dot(left, jnp.concatenate(windows, axis=0), preferred_element_type=jnp.float32)
            part = part.reshape(reps, rows, width)
            if g == 0:
                acc[side, :, :, width:] = jnp.zeros((reps, rows, cols - width), jnp.float32)
                acc[side, :, :, :width] = part
            else:
                acc[side, :, :, :width] += part
    code_rows(acc, table, own, (code1, code2, code3))


def multiply(table, h, chip_cols, t_parts, w_own, w_other):
    count, rows4, lanes = t_parts[0].shape
    rows = rows4 // SIDE
    depth, width = w_own.shape[1:]
    chips = SIDE * count
    code_shape = (2, rows, COLS)
    whole = pl.BlockSpec(memory_space=pl.ANY)
    return pl.pallas_call(
        functools.partial(product_kernel, h, chip_cols),
        grid_spec=pltpu.PrefetchScalarGridSpec(
            num_scalar_prefetch=1,
            grid=(1,),
            in_specs=[whole] * 6,
            out_specs=[pl.BlockSpec(code_shape, lambda k, tab: (0, 0, 0))] * 4,
            scratch_shapes=[
                pltpu.VMEM((chips, rows4, lanes), jnp.bfloat16),
                pltpu.VMEM((2, depth + 16, width), jnp.bfloat16),
                pltpu.VMEM((2, SIDE, rows, COLS), jnp.float32),
                pltpu.SemaphoreType.DMA((chips,)),
                pltpu.SemaphoreType.DMA((5, 2)),
            ],
        ),
        out_shape=[jax.ShapeDtypeStruct(code_shape, jnp.float32)] + [jax.ShapeDtypeStruct(code_shape, jnp.int16)] * 3,
        compiler_params=PARAMS,
        cost_estimate=pl.CostEstimate(
            flops=2 * rows4 * depth * 2 * width, bytes_accessed=2 * depth * width * 2 * 3, transcendentals=0
        ),
    )(table, *t_parts, w_own, w_other)


def finish_kernel(own, code1, code2, code3, rows_e, cols_e, out_own, out_other):
    cols = own.shape[2]
    for side, out in enumerate((out_own, out_other)):
        total = own[side]
        for code in (code1, code2, code3):
            whole = code[side].astype(jnp.int32).astype(jnp.float32)
            level = whole[:, cols - 1 :]
            total = total + whole * (jnp.exp2(level * (1.0 / STEPS)) * (1.0 / TOP))
        denominator = rows_e[:, 0:1] + cols_e[side, 0:1, :] - rows_e[:, 1:2] - cols_e[side, 1:2, :]
        out[...] = (total / denominator).astype(jnp.bfloat16)[:, : out.shape[1]]


def finish(own, codes, rows_e, cols_e, width):
    rows = own.shape[1]
    return pl.pallas_call(
        finish_kernel,
        out_shape=[jax.ShapeDtypeStruct((rows, width), jnp.bfloat16)] * 2,
        compiler_params=PARAMS,
        cost_estimate=pl.CostEstimate(flops=10 * own.size, bytes_accessed=2_000_000, transcendentals=0),
    )(own, *codes, rows_e, cols_e)


def row_energies(my_h, slab_energy, slab_irrep, virt_energy):
    irreps = virt_energy.shape[0]
    here = slab_energy.shape[0] // SIDE
    start = lax.axis_index("rep") * here
    energy_i = lax.dynamic_slice_in_dim(slab_energy, start, here)
    labels = lax.dynamic_slice_in_dim(slab_irrep, start, here)
    a_irrep = jnp.bitwise_xor(labels[None, :], my_h[:, None])
    hits = a_irrep[:, :, None] == jnp.arange(irreps, dtype=jnp.int32)
    energy_a = jnp.sum(jnp.where(hits[..., None], virt_energy[None, None], 0.0), axis=2)
    energy_i = jnp.broadcast_to(energy_i[None, :, None], energy_a.shape)
    return jnp.stack([energy_i, energy_a], axis=3).reshape(my_h.shape[0], -1, 2)


def col_energies(my_h, con, width, occ_energy, virt_energy):
    irreps, occ_width = occ_energy.shape
    virt_width = virt_energy.shape[1]
    columns = con * width + jnp.arange(COLS, dtype=jnp.int32)
    pair_index = columns // virt_width
    virt_index = columns % virt_width
    pair_irrep = pair_index // occ_width
    hits_j = pair_index[:, None] == jnp.arange(irreps * occ_width, dtype=jnp.int32)
    energy_j = jnp.sum(jnp.where(hits_j, occ_energy.reshape(-1), 0.0), axis=1)
    b_index = jnp.bitwise_xor(pair_irrep[None, :], my_h[:, None]) * virt_width + virt_index[None, :]
    hits_b = b_index[..., None] == jnp.arange(irreps * virt_width, dtype=jnp.int32)
    energy_b = jnp.sum(jnp.where(hits_b, virt_energy.reshape(-1), 0.0), axis=2)
    inside = jnp.arange(COLS) < width
    energy_j = jnp.broadcast_to(jnp.where(inside, energy_j, -1.0)[None], energy_b.shape)
    return jnp.stack([energy_j, energy_b], axis=1)


def shards(amplitudes, block_table, intermediate, slab_energy, slab_irrep, occ_energy, virt_energy):
    blocks, slab, virt, shard = amplitudes.shape
    width = intermediate.shape[2]
    rows = slab * virt
    per_rep = rows // SIDE
    mine = blocks // 2
    rep, con = lax.axis_index("rep"), lax.axis_index("con")
    core, chip = con % 2, con // 2
    y, x = chip // SIDE, chip % SIDE
    pair_width = occ_energy.shape[1] * virt_energy.shape[1]

    group = (rep * 2 * SIDE * SIDE + con) * shard // pair_width
    keep = lax.dynamic_index_in_dim(block_table, group, axis=1, keepdims=False).astype(jnp.bfloat16)
    masked = amplitudes * keep[:, None, None, None]
    masked = masked.reshape(blocks, rows, shard)
    kept = lax.dynamic_slice_in_dim(masked, core * mine, mine)
    given = lax.dynamic_slice_in_dim(masked, (1 - core) * mine, mine)
    got = swap_cores(given)
    intermediate = after(intermediate, got)
    t = jnp.where(core == 0, jnp.concatenate([kept, got], axis=2), jnp.concatenate([got, kept], axis=2))
    t = jnp.pad(t, ((0, 0), (0, 0), (0, 2 * SHARD - 2 * shard)))
    near = (jnp.array(OFFSETS, jnp.int32)[None, :], jnp.array(OFFSETS, jnp.int32)[:, None])
    x_chip = jnp.where(core == 0, near[0], near[1])
    y_chip = jnp.where(core == 0, near[1], near[0])
    chips = jnp.mod(y + y_chip, SIDE) * SIDE + jnp.mod(x + x_chip, SIDE)
    table = jnp.concatenate(
        [chips.reshape(-1), core[None], jnp.mod(rep + jnp.arange(SIDE, dtype=jnp.int32), SIDE)]
    ).astype(jnp.int32)

    my_h = core * mine + jnp.arange(mine, dtype=jnp.int32)
    rows_e = row_energies(my_h, slab_energy, slab_irrep, virt_energy)
    cols_e = jnp.stack(
        [col_energies(my_h, c, width, occ_energy, virt_energy) for c in (con, jnp.bitwise_xor(con, 1))], axis=1
    )

    table = after(table, rows_e, cols_e)
    known = {}

    def tied(name, value):
        return after(value, *[node(other) for other in TIES[name]]) if name in TIES else value

    def node(name):
        if name not in known:
            known[name] = build(name)
        return known[name]

    def build(name):
        kind, k = name[:-1], int(name[-1])
        if kind == "w":
            return swap_cores(tied(name, intermediate))
        if kind == "t":
            return t[k]
        if kind == "both":
            return ring(tied(name, t), 0, 1 if k == 0 else -1)
        if kind == "side":
            return ring(tied(name, node(f"both{k}")[k]), 0, 1 if k == 0 else -1)
        if kind == "row":
            row = jnp.stack([t[k], node("both0")[k], node("both1")[k], node(f"side{k}")])
            return row.reshape(SIDE, SIDE, per_rep, 2 * SHARD)
        h, first, last = CHUNKS[k]
        if kind == "here":
            return node(f"row{h}")[:, :, first:last].reshape(SIDE, -1, 2 * SHARD)
        if kind == "plus":
            return ring(tied(name, node(f"here{k}")), 1, 1)
        if kind == "minus":
            return ring(tied(name, node(f"here{k}")), 1, -1)
        if kind == "far":
            return ring(tied(name, node(f"plus{k}" if h == 0 else f"minus{k}")), 1, 1 if h == 0 else -1)
        if kind == "all":
            parts = [node(f"{part}{k}") for part in ("here", "plus", "minus", "far")]
            return multiply(tied(name, table), h, 2 * shard, parts, intermediate, node("w0"))
        if kind == "own":
            return node(f"all{k}")[0]
        if kind[:-1] == "code":
            hop = int(kind[-1])
            return to_replica(tied(name, node(f"all{k}")[hop]), hop)
        codes = [node(f"code{hop}{k}") for hop in (1, 2, 3)]
        return finish(tied(name, node(f"own{k}")), codes, rows_e[h, first:last], cols_e[h], width)

    done = {}
    for k, (h, first, last) in enumerate(CHUNKS):
        out_own, out_other = node(f"end{k}")
        done[h, first] = out_own, swap_cores(out_other)
    kept, got = [done[key][0] for key in sorted(done)], [done[key][1] for key in sorted(done)]
    kept, got = jnp.concatenate(kept), jnp.concatenate(got)
    out = jnp.where(core == 0, jnp.concatenate([kept, got]), jnp.concatenate([got, kept]))
    return out.reshape(blocks, slab // SIDE, virt, width)


def solution(mesh):
    placed = (P(None, None, None, ("rep", "con")), P(), P(None, "rep", "con"), P(), P(), P(), P())
    return jax.shard_map(
        shards, mesh=mesh, in_specs=placed, out_specs=P(None, "rep", None, "con"), check_vma=False
    )
```
